128 devices in a mesh: mpo: 8 (over z, core), sec: 16 (over x, y).
Axes of the slice: x: 4, y: 4, z: 4, core: 2. Of those that a mesh axis runs over, the one named last changes fastest.
Arguments:
- left_env: bfloat16 [256, 32, 384, 384], P('sec', 'mpo'), may hold values from -0.0546875 to 0.0546875
- site_tensor: bfloat16 [256, 384, 256], P('sec'), may hold values from -6 to 6
- mpo_column: bfloat16 [32, 4, 4], P('mpo'), may hold values from -3 to 3
- sector_slot: int32 [256], P('sec'), may hold values from 0 to 15, as said below
- kept: int32 [256], P('sec'), may hold values from 1 to 256
Outputs:
- expansion: bfloat16 [256, 384, 256], P('sec', 'mpo')
The draws below stay inside these ranges and needn't reach their ends.
Inputs may be any that keep to these rules, and one draw needn't show every extreme that they name: `sector_slot`: each aligned block of 16 entries holds every slot 0 to 15 once.
All inputs are finite; a program needn't handle non-finite values.
Results may differ from the reference program's by a relative error of at most 0.0053.
Values may be sent and summed in bfloat16 or wider, within the bound.
No kernel may reach another device: no remote copies, remote signals or barrier semaphores. Data moves between devices by JAX's collectives and lax.ppermute only.
A program may use at most 128 MiB of HBM per device.

```python
import jax
import jax.numpy as jnp
from jax import lax

PHYS = 4
DB = 384
ITERS = 6
GRP = 1
W = 32
XB = 256
SEC_DEV = 16
NSEC = 256


def draw_sector_slot(key, part):
    key = jax.random.fold_in(key, 11)
    blocks = NSEC // SEC_DEV
    keys = jax.random.split(key, blocks)

    def single_block(block_key):
        return jax.random.permutation(block_key, SEC_DEV)
    perms = jax.vmap(single_block)(keys)
    return perms.reshape(NSEC).astype(jnp.int32)


def set_ends(array, own_key, least, high):
    index_at = [jax.random.randint(jax.random.fold_in(own_key, axis), (), 0, length) for axis, length in enumerate(array.shape)]
    main_axis = array.shape.index(max(array.shape))
    beside = index_at[:main_axis] + [(index_at[main_axis] + 1) % array.shape[main_axis]] + index_at[main_axis + 1:]
    return array.at[tuple(index_at)].set(least).at[tuple(beside)].set(high)


def level_of(key, extent, pieces, least, largest):
    level, own = 1.0, jax.random.fold_in(key, 6)
    for dim, parts in pieces:
        draws = jnp.exp(jax.random.uniform(jax.random.fold_in(own, dim), (parts,), jnp.float32, least / len(pieces), largest / len(pieces)))
        level = level * jnp.repeat(draws, extent[dim] // parts).reshape([-1 if axis == dim else 1 for axis in range(len(extent))])
    return level


def normal_values(rng, extent, spread, reach, cuts=(), held_as=jnp.bfloat16):
    factor_of = level_of(rng, extent, cuts, -0.22, 0.18) if cuts else 1.0
    drawn = jax.random.normal(rng, extent, jnp.float32) * spread * factor_of
    return jnp.minimum(jnp.maximum(drawn, -reach), reach).astype(held_as)


def setup_inputs(seed: int = 0) -> dict:
    splits = jax.random.split(jax.random.key(seed), 6)
    left_env = normal_values(splits[0], (NSEC, W, DB, DB), (W * DB) ** -0.5, 0.0546875, ((0, 16), (1, 8)))
    site_tensor = normal_values(splits[1], (NSEC, DB, XB), 1.0, 6.0, ((0, 16),))
    mpo_column = normal_values(splits[2], (W, PHYS, PHYS), PHYS ** -0.5, 3.0, ((0, 8),))
    sector_slot = draw_sector_slot(jax.random.fold_in(splits[5], 71), 0)
    kept = set_ends(jax.random.randint(splits[4], (NSEC,), 1, XB + 1), jax.random.fold_in(splits[4], 1), 1, XB).astype(jnp.int32)
    return {"left_env": left_env, "site_tensor": site_tensor, "mpo_column": mpo_column, "sector_slot": sector_slot, "kept": kept}


def batch_product(first, second):
    return jnp.einsum('kab,kbc->kac', first, second, precision=lax.Precision.HIGHEST)

def inverse_root(gram):
    columns = gram.shape[-1]
    frobenius = jnp.sqrt(lax.optimization_barrier(jnp.sum(gram * gram, axis=(1, 2))))
    current = gram / frobenius[:, None, None]
    identity = jnp.broadcast_to(jnp.eye(columns, dtype=jnp.float32), gram.shape)
    partner = identity
    for repeat in range(ITERS):
        factor = 1.5 * identity - 0.5 * batch_product(partner, current)
        current = batch_product(current, factor)
        partner = batch_product(factor, partner)
    return partner / jnp.sqrt(frobenius)[:, None, None]

def reference(left_env, site_tensor, mpo_column, sector_slot, kept):
    total_sec, row_count, col_count = site_tensor.shape
    phys_dim = mpo_column.shape[1]
    right_dim = col_count // phys_dim
    mpo_wide = mpo_column.astype(jnp.float32)

    def one_sector(blocks):
        left_block, site_block = blocks
        shaped = site_block.astype(jnp.float32).reshape(row_count, phys_dim, right_dim)
        mixed_site = jnp.einsum('asb,wst->watb', shaped, mpo_wide).astype(jnp.bfloat16)
        mixed_site = mixed_site.reshape(W, row_count, col_count)
        return jnp.einsum('wab,wbc->ac', left_block.astype(jnp.float32), mixed_site.astype(jnp.float32))
    terms = lax.map(one_sector, (left_env, site_tensor))
    sector_ids = jnp.arange(total_sec, dtype=jnp.int32)
    source_block = (sector_ids // SEC_DEV).astype(jnp.int32)
    target = (sector_slot // GRP * SEC_DEV + source_block * GRP + sector_slot % GRP).astype(jnp.int32)
    routed = jnp.zeros_like(terms).at[target].set(terms)
    gram = jnp.einsum('kac,kad->kcd', routed, routed, precision=lax.Precision.HIGHEST)
    root_factor = inverse_root(gram)
    kept_mask = (jnp.arange(col_count, dtype=jnp.int32)[None, :] < kept[:, None]).astype(jnp.float32)
    result = batch_product(routed, root_factor) * kept_mask[:, None, :]
    return result.astype(jnp.bfloat16)
```

```python
import functools

import jax
import jax.numpy as jnp
from jax import lax
from jax.experimental import pallas as pl
from jax.experimental.pallas import tpu as pltpu
from jax.sharding import PartitionSpec as P

ITERS = 6
F32, BF16 = jnp.float32, jnp.bfloat16


def mixing_matrix(mpo_ref, out_ref, wslices, phys, right):
    per = 128 // right
    row = lax.broadcasted_iota(jnp.int32, (right, 128), 0)
    lane = lax.broadcasted_iota(jnp.int32, (right, 128), 1)
    for s in range(phys):
        for w in range(wslices):
            for t in range(0, phys, per):
                block = jnp.zeros((right, 128), F32)
                for p in range(per):
                    value = mpo_ref[(w * phys + s) * phys + t + p]
                    block = jnp.where(lane == row + p * right, value, block)
                column = (w * phys + t) * right
                out_ref[s * right : (s + 1) * right, column : column + 128] = block.astype(BF16)


def term_kernel(order_ref, mpo_ref, left_ref, site_ref, *rest, wslices, phys, right, adds):
    if adds:
        other_ref, out_ref, mix_ref = rest
    else:
        out_ref, mix_ref = rest
    columns = phys * right

    @pl.when(pl.program_id(0) == 0)
    def _():
        mixing_matrix(mpo_ref, mix_ref, wslices, phys, right)

    mixed = jnp.dot(site_ref[0], mix_ref[...], preferred_element_type=F32).astype(BF16)
    stacked = jnp.concatenate(
        [mixed[:, w * columns : (w + 1) * columns] for w in range(wslices)], axis=0
    )
    left = jnp.concatenate([left_ref[0, w] for w in range(wslices)], axis=1)
    term = jnp.dot(left, stacked, preferred_element_type=F32)
    if adds:
        term = term + other_ref[0].astype(F32)
    out_ref[0] = term.astype(out_ref.dtype)


def terms(order, mpo_flat, left_env, site, other, out_dtype):
    count = order.shape[0]
    _, wslices, rows, _ = left_env.shape
    columns = site.shape[2]
    phys = 4
    right = columns // phys
    in_specs = [
        pl.BlockSpec((1, wslices, rows, rows), lambda j, o, m: (o[j], 0, 0, 0)),
        pl.BlockSpec((1, rows, columns), lambda j, o, m: (o[j], 0, 0)),
    ]
    operands = [left_env, site]
    if other is not None:
        in_specs.append(pl.BlockSpec((1, rows, columns), lambda j, o, m: (j, 0, 0)))
        operands.append(other)
    flops = 2 * count * rows * columns * wslices * (rows + columns)
    moved = count * (wslices * rows * rows * 2 + rows * columns * 6)
    return pl.pallas_call(
        functools.partial(
            term_kernel, wslices=wslices, phys=phys, right=right, adds=other is not None
        ),
        out_shape=jax.ShapeDtypeStruct((count, rows, columns), out_dtype),
        grid_spec=pltpu.PrefetchScalarGridSpec(
            num_scalar_prefetch=2,
            grid=(count,),
            in_specs=in_specs,
            out_specs=pl.BlockSpec((1, rows, columns), lambda j, o, m: (j, 0, 0)),
            scratch_shapes=[pltpu.VMEM((columns, wslices * columns), BF16)],
        ),
        compiler_params=pltpu.CompilerParams(vmem_limit_bytes=24 * 2**20),
        cost_estimate=pl.CostEstimate(flops=flops, bytes_accessed=moved, transcendentals=0),
    )(order, mpo_flat, *operands)


def split(a):
    high = a.astype(BF16)
    return high, (a - high.astype(F32)).astype(BF16)


def product(a, b):
    return jnp.dot(
        jnp.concatenate([a[0], a[0], a[1]], axis=1),
        jnp.concatenate([b[0], b[1], b[0]], axis=0),
        preferred_element_type=F32,
    )


def root_kernel(own_ref, far_ref, up_ref, down_ref, out_ref):
    count, rows, columns = own_ref.shape
    parts, _, part_rows, _ = out_ref.shape
    eye = lax.broadcasted_iota(jnp.int32, (columns, columns), 0) == lax.broadcasted_iota(
        jnp.int32, (columns, columns), 1
    )
    identity = eye.astype(F32)
    sectors = range(count)
    term, current, scale = [], [], []
    for b in sectors:
        total = (
            own_ref[b]
            + far_ref[b].astype(F32)
            + up_ref[b].astype(F32)
            + down_ref[b].astype(F32)
        )
        high, low = split(total)
        gram = lax.dot_general(
            jnp.concatenate([high, high, low], axis=0),
            jnp.concatenate([high, low, high], axis=0),
            (((0,), (0,)), ((), ())),
            preferred_element_type=F32,
        )
        norm = jnp.sqrt(jnp.sum(gram * gram, keepdims=True))
        term.append((high, low))
        current.append(gram / norm)
        scale.append(1.0 / jnp.sqrt(norm))
    partner = [None] * count
    for repeat in range(ITERS):
        halves = [split(current[b]) for b in sectors]
        if repeat == 0:
            factor = [1.5 * identity - 0.5 * current[b] for b in sectors]
        else:
            others = [split(partner[b]) for b in sectors]
            factor = [1.5 * identity - 0.5 * product(others[b], halves[b]) for b in sectors]
        pairs = [split(factor[b]) for b in sectors]
        if repeat < ITERS - 1:
            current = [product(halves[b], pairs[b]) for b in sectors]
        if repeat == 0:
            partner = factor
        else:
            partner = [product(pairs[b], others[b]) for b in sectors]
    for b in sectors:
        result = (product(term[b], split(partner[b] * scale[b]))).astype(BF16)
        for m in range(parts):
            out_ref[m, b] = result[m * part_rows : (m + 1) * part_rows]


def expansions(own, far, up, down, parts):
    count, rows, columns = own.shape
    flops = 2 * 3 * count * columns * columns * (15 * columns + 2 * rows)
    return pl.pallas_call(
        root_kernel,
        out_shape=jax.ShapeDtypeStruct((parts, count, rows // parts, columns), BF16),
        in_specs=[pl.BlockSpec(memory_space=pltpu.VMEM)] * 4,
        out_specs=pl.BlockSpec(memory_space=pltpu.VMEM),
        compiler_params=pltpu.CompilerParams(vmem_limit_bytes=40 * 2**20),
        cost_estimate=pl.CostEstimate(
            flops=flops, bytes_accessed=count * rows * columns * 12, transcendentals=0
        ),
    )(own, far, up, down)


def shards(left_env, site_tensor, mpo_column, sector_slot, kept):
    columns = site_tensor.shape[2]
    members = lax.axis_size("mpo")
    chips = members // 2
    me = lax.axis_index("mpo")
    chip, core = me // 2, me % 2

    positions = jnp.arange(sector_slot.shape[0], dtype=jnp.int32)

    def order_of(targets):
        slots = jnp.stack([2 * (2 * (c % chips) + q) + b for c, q in targets for b in range(2)])
        match = sector_slot[None, :] == slots[:, None]
        return jnp.sum(jnp.where(match, positions[None, :], 0), axis=1, dtype=jnp.int32)

    mpo_flat = mpo_column.astype(F32).reshape(-1)
    other = 1 - core
    order = order_of(
        [
            (chip + 2, other),
            (chip + 1, other),
            (chip + 3, other),
            (chip + 2, core),
            (chip + 1, core),
            (chip + 3, core),
            (chip, other),
            (chip, core),
        ]
    )
    swap = [(2 * c + q, 2 * c + 1 - q) for c in range(chips) for q in range(2)]

    def shift(step):
        return [
            (2 * c + q, 2 * ((c + step) % chips) + q) for c in range(chips) for q in range(2)
        ]

    def run(first, count, recv, dtype):
        return terms(order[first : first + count], mpo_flat, left_env, site_tensor, recv, dtype)

    far_other = lax.ppermute(run(0, 2, None, BF16), "mpo", swap)
    near_other = lax.ppermute(run(2, 4, None, BF16), "mpo", swap)
    far = lax.ppermute(run(6, 2, far_other, BF16), "mpo", shift(2))
    near = run(8, 4, near_other, BF16)
    up = lax.ppermute(near[:2], "mpo", shift(1))
    down = lax.ppermute(near[2:], "mpo", shift(3))
    own_other = lax.ppermute(run(12, 2, None, BF16), "mpo", swap)
    own = run(14, 2, own_other, F32)
    result = expansions(own, far, up, down, members)
    rows = lax.all_to_all(result, "mpo", split_axis=0, concat_axis=0, tiled=True)
    rows = rows.reshape(-1, rows.shape[2], columns)
    routed = lax.all_to_all(rows, "sec", split_axis=0, concat_axis=0, tiled=True)
    keep = jnp.arange(columns, dtype=jnp.int32)[None, None, :] < kept[:, None, None]
    return jnp.where(keep, routed, jnp.zeros((), BF16))


def solution(mesh):
    return jax.shard_map(
        shards,
        mesh=mesh,
        in_specs=(
            P("sec", "mpo", None, None),
            P("sec", None, None),
            P("mpo", None, None),
            P("sec"),
            P("sec"),
        ),
        out_specs=P("sec", "mpo", None),
        check_vma=False,
    )
```

```python
import functools

import jax
import jax.numpy as jnp
from jax import lax
from jax.experimental import pallas as pl
from jax.experimental.pallas import tpu as pltpu
from jax.sharding import PartitionSpec as P

ITERS = 6
EARLY = 4
PHYS = 4
CHIPS = 4
TERM_MIB = 57
F32, BF16 = jnp.float32, jnp.bfloat16


def mixing_matrix(mpo_ref, out_ref, wslices, phys, right):
    per = 128 // right
    row = lax.broadcasted_iota(jnp.int32, (right, 128), 0)
    lane = lax.broadcasted_iota(jnp.int32, (right, 128), 1)
    for s in range(phys):
        for w in range(wslices):
            for t in range(0, phys, per):
                block = jnp.zeros((right, 128), F32)
                for p in range(per):
                    value = mpo_ref[(w * phys + s) * phys + t + p]
                    block = jnp.where(lane == row + p * right, value, block)
                column = (w * phys + t) * right
                out_ref[s * right : (s + 1) * right, column : column + 128] = block.astype(BF16)


def mix(site, mix_ref, stacked_ref):
    rows, columns = site.shape
    for w in range(stacked_ref.shape[0] // rows):
        stacked_ref[w * rows : (w + 1) * rows] = jnp.dot(
            site, mix_ref[:, w * columns : (w + 1) * columns], preferred_element_type=F32
        ).astype(BF16)


def contract(left_ref, stacked_ref):
    left = jnp.concatenate([left_ref[w] for w in range(left_ref.shape[0])], axis=1)
    return jnp.dot(left, stacked_ref[...], preferred_element_type=F32)


def term_kernel(me_ref, slot_ref, mpo_ref, left_hbm, site_hbm, *rest, groups):
    added = sum(offset is not None for _, _, offset in groups)
    others, outs = list(rest[:added]), rest[added : added + len(groups)]
    left_ref, site_ref, mix_ref, stacked_ref, inverse_ref, left_sem, site_sem = rest[
        added + len(groups) :
    ]
    wslices = left_ref.shape[1]
    columns = site_ref.shape[2]
    chip, core = lax.div(me_ref[0], 2), lax.rem(me_ref[0], 2)
    for k in range(slot_ref.shape[0]):
        inverse_ref[slot_ref[k]] = k
    work = []
    for g, (targets, _, offset) in enumerate(groups):
        other = None if offset is None else others.pop(0)
        for j, (step, flip) in enumerate(targets):
            member = 2 * lax.rem(chip + step, CHIPS) + (1 - core if flip else core)
            copies = []
            for b in range(2):
                n = 2 * len(work) + b
                sector = inverse_ref[2 * member + b]
                copies.append(
                    pltpu.make_async_copy(site_hbm.at[sector], site_ref.at[n], site_sem.at[n])
                )
                copies.append(
                    pltpu.make_async_copy(left_hbm.at[sector], left_ref.at[n], left_sem.at[n])
                )
            for copy in copies:
                copy.start()
            work.append((copies, outs[g], other, offset, 2 * j))
    mixing_matrix(mpo_ref, mix_ref, wslices, PHYS, columns // PHYS)
    for i, (copies, out_ref, other_ref, offset, start) in enumerate(work):
        for copy in copies:
            copy.wait()
        for b in range(2):
            mix(site_ref[2 * i + b], mix_ref, stacked_ref.at[b])
        for b in range(2):
            term = contract(left_ref.at[2 * i + b], stacked_ref.at[b])
            if other_ref is not None:
                term = term + other_ref[offset + start + b].astype(F32)
            out_ref[start + b] = term.astype(out_ref.dtype)


def terms(me, slots, mpo_flat, left_env, site, *groups):
    sectors, wslices, rows, _ = left_env.shape
    columns = site.shape[2]
    count = 2 * sum(len(targets) for targets, _, _ in groups)
    vmem = pl.BlockSpec(memory_space=pltpu.VMEM)
    smem = pl.BlockSpec(memory_space=pltpu.SMEM)
    hbm = pl.BlockSpec(memory_space=pltpu.HBM)
    others = [other[0] for _, _, other in groups if other is not None]
    flops = 2 * count * rows * columns * wslices * (rows + columns)
    moved = count * (wslices * rows * rows * 2 + rows * columns * 2)
    return pl.pallas_call(
        functools.partial(
            term_kernel,
            groups=[(targets, dtype, other and other[1]) for targets, dtype, other in groups],
        ),
        out_shape=[
            jax.ShapeDtypeStruct((2 * len(targets), rows, columns), dtype)
            for targets, dtype, _ in groups
        ],
        in_specs=[smem, smem, smem, hbm, hbm] + [vmem] * len(others),
        out_specs=[vmem] * len(groups),
        scratch_shapes=[
            pltpu.VMEM((count, wslices, rows, rows), BF16),
            pltpu.VMEM((count, rows, columns), BF16),
            pltpu.VMEM((columns, wslices * columns), BF16),
            pltpu.VMEM((2, wslices * rows, columns), BF16),
            pltpu.SMEM((sectors,), jnp.int32),
            pltpu.SemaphoreType.DMA((count,)),
            pltpu.SemaphoreType.DMA((count,)),
        ],
        compiler_params=pltpu.CompilerParams(vmem_limit_bytes=TERM_MIB * 2**20),
        cost_estimate=pl.CostEstimate(flops=flops, bytes_accessed=moved, transcendentals=0),
    )(me, slots, mpo_flat, left_env, site, *others)


def split(a):
    high = a.astype(BF16)
    return high, (a - high.astype(F32)).astype(BF16)


def product(a, b):
    return jnp.dot(
        jnp.concatenate([a[0], a[0], a[1]], axis=1),
        jnp.concatenate([b[0], b[1], b[0]], axis=0),
        preferred_element_type=F32,
    )


def root_kernel(own_ref, other_ref, far_ref, up_ref, down_ref, out_ref):
    count, rows, columns = far_ref.shape
    parts, _, part_rows, _ = out_ref.shape
    eye = lax.broadcasted_iota(jnp.int32, (columns, columns), 0) == lax.broadcasted_iota(
        jnp.int32, (columns, columns), 1
    )
    identity = eye.astype(F32)
    sectors = range(count)
    term, current, scale = [], [], []
    for b in sectors:
        total = (
            own_ref[b]
            + other_ref[b].astype(F32)
            + far_ref[b].astype(F32)
            + up_ref[b].astype(F32)
            + down_ref[b].astype(F32)
        )
        high, low = split(total)
        gram = lax.dot_general(
            jnp.concatenate([high, high, low], axis=0),
            jnp.concatenate([high, low, high], axis=0),
            (((0,), (0,)), ((), ())),
            preferred_element_type=F32,
        )
        norm = jnp.sqrt(jnp.sum(gram * gram, keepdims=True))
        term.append((high, low))
        current.append(gram / norm)
        scale.append(1.0 / jnp.sqrt(norm))
    partner = [None] * count
    for repeat in range(ITERS):
        if repeat < EARLY:
            rounded = [current[b].astype(BF16) for b in sectors]
            if repeat == 0:
                step = current
            else:
                others = [partner[b].astype(BF16) for b in sectors]
                step = [
                    jnp.dot(others[b], rounded[b], preferred_element_type=F32) for b in sectors
                ]
            small = [step[b].astype(BF16) for b in sectors]
            current = [
                1.5 * current[b]
                - 0.5 * jnp.dot(rounded[b], small[b], preferred_element_type=F32)
                for b in sectors
            ]
            if repeat == 0:
                partner = [1.5 * identity - 0.5 * step[b] for b in sectors]
            else:
                partner = [
                    1.5 * partner[b]
                    - 0.5 * jnp.dot(small[b], others[b], preferred_element_type=F32)
                    for b in sectors
                ]
        else:
            halves = [split(current[b]) for b in sectors]
            others = [split(partner[b]) for b in sectors]
            factor = [1.5 * identity - 0.5 * product(others[b], halves[b]) for b in sectors]
            pairs = [split(factor[b]) for b in sectors]
            if repeat < ITERS - 1:
                current = [product(halves[b], pairs[b]) for b in sectors]
            partner = [product(pairs[b], others[b]) for b in sectors]
    for b in sectors:
        result = (product(term[b], split(partner[b] * scale[b]))).astype(BF16)
        for m in range(parts):
            out_ref[m, b] = result[m * part_rows : (m + 1) * part_rows]


def expansions(own, other, far, up, down, parts):
    count, rows, columns = far.shape
    flops = 2 * 3 * count * columns * columns * (15 * columns + 2 * rows)
    return pl.pallas_call(
        root_kernel,
        out_shape=jax.ShapeDtypeStruct((parts, count, rows // parts, columns), BF16),
        in_specs=[pl.BlockSpec(memory_space=pltpu.VMEM)] * 5,
        out_specs=pl.BlockSpec(memory_space=pltpu.VMEM),
        compiler_params=pltpu.CompilerParams(vmem_limit_bytes=40 * 2**20),
        cost_estimate=pl.CostEstimate(
            flops=flops, bytes_accessed=count * rows * columns * 12, transcendentals=0
        ),
    )(own, other, far, up, down)


def shards(left_env, site_tensor, mpo_column, sector_slot, kept):
    columns = site_tensor.shape[2]
    members = lax.axis_size("mpo")
    me = lax.axis_index("mpo").reshape(1)
    swap = [(2 * c + q, 2 * c + 1 - q) for c in range(CHIPS) for q in range(2)]

    def shift(step):
        return [
            (2 * c + q, 2 * ((c + step) % CHIPS) + q) for c in range(CHIPS) for q in range(2)
        ]

    flat = mpo_column.astype(F32).reshape(-1)
    after = lax.optimization_barrier

    def run(slots, *groups):
        return terms(me, slots, flat, left_env, site_tensor, *groups)

    far_other, near_other, far_own = run(
        sector_slot,
        ([(2, 1)], BF16, None),
        ([(1, 1), (3, 1)], BF16, None),
        ([(2, 0)], F32, None),
    )
    far_other = lax.ppermute(far_other, "mpo", swap)
    near_other, far_other = after((near_other, far_other))
    near_other = lax.ppermute(near_other, "mpo", swap)
    far = (far_own + far_other.astype(F32)).astype(BF16)
    far = lax.ppermute(far, "mpo", shift(2))
    up, down, own_other = run(
        sector_slot,
        ([(1, 0)], BF16, (near_other, 0)),
        ([(3, 0)], BF16, (near_other, 2)),
        ([(0, 1)], BF16, None),
    )
    up, slots = after((up, sector_slot))
    up = lax.ppermute(up, "mpo", shift(1))
    down = lax.ppermute(down, "mpo", shift(3))
    own_other = lax.ppermute(own_other, "mpo", swap)
    (own,) = run(slots, ([(0, 0)], F32, None))
    result = expansions(own, own_other, far, up, down, members)
    rows = lax.all_to_all(result, "mpo", split_axis=0, concat_axis=0, tiled=True)
    rows = rows.reshape(-1, rows.shape[2], columns)
    routed = lax.all_to_all(rows, "sec", split_axis=0, concat_axis=0, tiled=True)
    keep = jnp.arange(columns, dtype=jnp.int32)[None, None, :] < kept[:, None, None]
    return jnp.where(keep, routed, jnp.zeros((), BF16))


def solution(mesh):
    return jax.shard_map(
        shards,
        mesh=mesh,
        in_specs=(
            P("sec", "mpo", None, None),
            P("sec", None, None),
            P("mpo", None, None),
            P("sec"),
            P("sec"),
        ),
        out_specs=P("sec", "mpo", None),
        check_vma=False,
    )
```

```python
import functools

import jax
import jax.numpy as jnp
from jax import lax
from jax.experimental import pallas as pl
from jax.experimental.pallas import tpu as pltpu
from jax.sharding import PartitionSpec as P

ITERS = 6
EARLY = 4
PHYS = 4
CHIPS = 4
TERM_MIB = 48
F32, BF16 = jnp.float32, jnp.bfloat16


def mixing_matrix(mpo_ref, out_ref, wslices, phys, right):
    per = 128 // right
    row = lax.broadcasted_iota(jnp.int32, (right, 128), 0)
    lane = lax.broadcasted_iota(jnp.int32, (right, 128), 1)
    for s in range(phys):
        for w in range(wslices):
            for t in range(0, phys, per):
                block = jnp.zeros((right, 128), F32)
                for p in range(per):
                    value = mpo_ref[(w * phys + s) * phys + t + p]
                    block = jnp.where(lane == row + p * right, value, block)
                column = (w * phys + t) * right
                out_ref[s * right : (s + 1) * right, column : column + 128] = block.astype(BF16)


def mix(site, mix_ref, stacked_ref):
    rows, columns = site.shape
    for w in range(stacked_ref.shape[0] // rows):
        stacked_ref[w * rows : (w + 1) * rows] = jnp.dot(
            site, mix_ref[:, w * columns : (w + 1) * columns], preferred_element_type=F32
        ).astype(BF16)


def contract(left_ref, stacked_ref):
    left = jnp.concatenate([left_ref[w] for w in range(left_ref.shape[0])], axis=1)
    return jnp.dot(left, stacked_ref[...], preferred_element_type=F32)


def term_kernel(me_ref, slot_ref, mpo_ref, left_hbm, site_ref, *rest, groups):
    added = sum(offset is not None for _, _, offset in groups)
    others, outs = list(rest[:added]), rest[added : added + len(groups)]
    left_ref, mix_ref, stacked_ref, inverse_ref, left_sem = rest[added + len(groups) :]
    wslices = left_ref.shape[1]
    columns = site_ref.shape[2]
    chip, core = lax.div(me_ref[0], 2), lax.rem(me_ref[0], 2)
    for k in range(slot_ref.shape[0]):
        inverse_ref[slot_ref[k]] = k
    work = []
    for g, (targets, _, offset) in enumerate(groups):
        other = None if offset is None else others.pop(0)
        for j, (step, flip) in enumerate(targets):
            member = 2 * lax.rem(chip + step, CHIPS) + (1 - core if flip else core)
            parts = []
            for b in range(2):
                n = 2 * len(work) + b
                sector = inverse_ref[2 * member + b]
                copy = pltpu.make_async_copy(left_hbm.at[sector], left_ref.at[n], left_sem.at[n])
                copy.start()
                parts.append((copy, sector))
            work.append((parts, outs[g], other, offset, 2 * j))
    mixing_matrix(mpo_ref, mix_ref, wslices, PHYS, columns // PHYS)
    for i, (parts, out_ref, other_ref, offset, start) in enumerate(work):
        for copy, _ in parts:
            copy.wait()
        for b, (_, sector) in enumerate(parts):
            mix(site_ref[sector], mix_ref, stacked_ref.at[b])
        for b in range(2):
            term = contract(left_ref.at[2 * i + b], stacked_ref.at[b])
            if other_ref is not None:
                term = term + other_ref[offset + start + b].astype(F32)
            out_ref[start + b] = term.astype(out_ref.dtype)


def terms(me, slots, mpo_flat, left_env, site, *groups):
    sectors, wslices, rows, _ = left_env.shape
    columns = site.shape[2]
    count = 2 * sum(len(targets) for targets, _, _ in groups)
    vmem = pl.BlockSpec(memory_space=pltpu.VMEM)
    smem = pl.BlockSpec(memory_space=pltpu.SMEM)
    hbm = pl.BlockSpec(memory_space=pltpu.HBM)
    others = [other[0] for _, _, other in groups if other is not None]
    flops = 2 * count * rows * columns * wslices * (rows + columns)
    moved = count * (wslices * rows * rows * 2 + rows * columns * 2)
    return pl.pallas_call(
        functools.partial(
            term_kernel,
            groups=[(targets, dtype, other and other[1]) for targets, dtype, other in groups],
        ),
        out_shape=[
            jax.ShapeDtypeStruct((2 * len(targets), rows, columns), dtype)
            for targets, dtype, _ in groups
        ],
        in_specs=[smem, smem, smem, hbm, vmem] + [vmem] * len(others),
        out_specs=[vmem] * len(groups),
        scratch_shapes=[
            pltpu.VMEM((count, wslices, rows, rows), BF16),
            pltpu.VMEM((columns, wslices * columns), BF16),
            pltpu.VMEM((2, wslices * rows, columns), BF16),
            pltpu.SMEM((sectors,), jnp.int32),
            pltpu.SemaphoreType.DMA((count,)),
        ],
        compiler_params=pltpu.CompilerParams(vmem_limit_bytes=TERM_MIB * 2**20),
        cost_estimate=pl.CostEstimate(flops=flops, bytes_accessed=moved, transcendentals=0),
    )(me, slots, mpo_flat, left_env, site, *others)


def split(a):
    high = a.astype(BF16)
    return high, (a - high.astype(F32)).astype(BF16)


def product(a, b):
    return jnp.dot(
        jnp.concatenate([a[0], a[0], a[1]], axis=1),
        jnp.concatenate([b[0], b[1], b[0]], axis=0),
        preferred_element_type=F32,
    )


def root_kernel(own_ref, other_ref, far_ref, up_ref, down_ref, out_ref):
    count, rows, columns = far_ref.shape
    parts, _, part_rows, _ = out_ref.shape
    eye = lax.broadcasted_iota(jnp.int32, (columns, columns), 0) == lax.broadcasted_iota(
        jnp.int32, (columns, columns), 1
    )
    identity = eye.astype(F32)
    sectors = range(count)
    term, current, scale = [], [], []
    for b in sectors:
        total = (
            own_ref[b]
            + other_ref[b].astype(F32)
            + far_ref[b].astype(F32)
            + up_ref[b].astype(F32)
            + down_ref[b].astype(F32)
        )
        high, low = split(total)
        gram = lax.dot_general(
            jnp.concatenate([high, high, low], axis=0),
            jnp.concatenate([high, low, high], axis=0),
            (((0,), (0,)), ((), ())),
            preferred_element_type=F32,
        )
        norm = jnp.sqrt(jnp.sum(gram * gram, keepdims=True))
        term.append((high, low))
        current.append(gram / norm)
        scale.append(1.0 / jnp.sqrt(norm))
    partner = [None] * count
    for repeat in range(ITERS):
        if repeat < EARLY:
            rounded = [current[b].astype(BF16) for b in sectors]
            if repeat == 0:
                step = current
            else:
                others = [partner[b].astype(BF16) for b in sectors]
                step = [
                    jnp.dot(others[b], rounded[b], preferred_element_type=F32) for b in sectors
                ]
            small = [step[b].astype(BF16) for b in sectors]
            current = [
                1.5 * current[b]
                - 0.5 * jnp.dot(rounded[b], small[b], preferred_element_type=F32)
                for b in sectors
            ]
            if repeat == 0:
                partner = [1.5 * identity - 0.5 * step[b] for b in sectors]
            else:
                partner = [
                    1.5 * partner[b]
                    - 0.5 * jnp.dot(small[b], others[b], preferred_element_type=F32)
                    for b in sectors
                ]
        else:
            halves = [split(current[b]) for b in sectors]
            others = [split(partner[b]) for b in sectors]
            factor = [1.5 * identity - 0.5 * product(others[b], halves[b]) for b in sectors]
            pairs = [split(factor[b]) for b in sectors]
            if repeat < ITERS - 1:
                current = [product(halves[b], pairs[b]) for b in sectors]
            partner = [product(pairs[b], others[b]) for b in sectors]
    for b in sectors:
        result = (product(term[b], split(partner[b] * scale[b]))).astype(BF16)
        for m in range(parts):
            out_ref[m, b] = result[m * part_rows : (m + 1) * part_rows]


def expansions(own, other, far, up, down, parts):
    count, rows, columns = far.shape
    flops = 2 * 3 * count * columns * columns * (15 * columns + 2 * rows)
    return pl.pallas_call(
        root_kernel,
        out_shape=jax.ShapeDtypeStruct((parts, count, rows // parts, columns), BF16),
        in_specs=[pl.BlockSpec(memory_space=pltpu.VMEM)] * 5,
        out_specs=pl.BlockSpec(memory_space=pltpu.VMEM),
        compiler_params=pltpu.CompilerParams(vmem_limit_bytes=40 * 2**20),
        cost_estimate=pl.CostEstimate(
            flops=flops, bytes_accessed=count * rows * columns * 12, transcendentals=0
        ),
    )(own, other, far, up, down)


def shards(left_env, site_tensor, mpo_column, sector_slot, kept):
    columns = site_tensor.shape[2]
    members = lax.axis_size("mpo")
    me = lax.axis_index("mpo").reshape(1)
    swap = [(2 * c + q, 2 * c + 1 - q) for c in range(CHIPS) for q in range(2)]

    def shift(step):
        return [
            (2 * c + q, 2 * ((c + step) % CHIPS) + q) for c in range(CHIPS) for q in range(2)
        ]

    flat = mpo_column.astype(F32).reshape(-1)
    after = lax.optimization_barrier

    def run(slots, *groups):
        return terms(me, slots, flat, left_env, site_tensor, *groups)

    far_other, near_other, far_own = run(
        sector_slot,
        ([(2, 1)], BF16, None),
        ([(1, 1), (3, 1)], BF16, None),
        ([(2, 0)], F32, None),
    )
    far_other = lax.ppermute(far_other, "mpo", swap)
    near_other, far_other = after((near_other, far_other))
    near_other = lax.ppermute(near_other, "mpo", swap)
    far = (far_own + far_other.astype(F32)).astype(BF16)
    far = lax.ppermute(far, "mpo", shift(2))
    up, down, own_other = run(
        sector_slot,
        ([(1, 0)], BF16, (near_other, 0)),
        ([(3, 0)], BF16, (near_other, 2)),
        ([(0, 1)], BF16, None),
    )
    up, slots = after((up, sector_slot))
    up = lax.ppermute(up, "mpo", shift(1))
    down = lax.ppermute(down, "mpo", shift(3))
    own_other = lax.ppermute(own_other, "mpo", swap)
    (own,) = run(slots, ([(0, 0)], F32, None))
    result = expansions(own, own_other, far, up, down, members)
    rows = lax.all_to_all(result, "mpo", split_axis=0, concat_axis=0, tiled=True)
    rows = rows.reshape(-1, rows.shape[2], columns)
    routed = lax.all_to_all(rows, "sec", split_axis=0, concat_axis=0, tiled=True)
    keep = jnp.arange(columns, dtype=jnp.int32)[None, None, :] < kept[:, None, None]
    return jnp.where(keep, routed, jnp.zeros((), BF16))


def solution(mesh):
    return jax.shard_map(
        shards,
        mesh=mesh,
        in_specs=(
            P("sec", "mpo", None, None),
            P("sec", None, None),
            P("mpo", None, None),
            P("sec"),
            P("sec"),
        ),
        out_specs=P("sec", "mpo", None),
        check_vma=False,
    )
```

```python
import functools

import jax
import jax.numpy as jnp
from jax import lax
from jax.experimental import pallas as pl
from jax.experimental.pallas import tpu as pltpu
from jax.sharding import PartitionSpec as P

ITERS = 6
EARLY = 4
PHYS = 4
CHIPS = 4
TERM_MIB = 48
F32, BF16 = jnp.float32, jnp.bfloat16


def mixing_matrix(mpo_ref, out_ref, wslices, phys, right):
    per = 128 // right
    row = lax.broadcasted_iota(jnp.int32, (right, 128), 0)
    lane = lax.broadcasted_iota(jnp.int32, (right, 128), 1)
    for s in range(phys):
        for w in range(wslices):
            for t in range(0, phys, per):
                block = jnp.zeros((right, 128), F32)
                for p in range(per):
                    value = mpo_ref[(w * phys + s) * phys + t + p]
                    block = jnp.where(lane == row + p * right, value, block)
                column = (w * phys + t) * right
                out_ref[s * right : (s + 1) * right, column : column + 128] = block.astype(BF16)


def mix(site, mix_ref, stacked_ref):
    rows, columns = site.shape
    for w in range(stacked_ref.shape[0] // rows):
        stacked_ref[w * rows : (w + 1) * rows] = jnp.dot(
            site, mix_ref[:, w * columns : (w + 1) * columns], preferred_element_type=F32
        ).astype(BF16)


def contract(left_ref, stacked_ref):
    left = jnp.concatenate([left_ref[w] for w in range(left_ref.shape[0])], axis=1)
    return jnp.dot(left, stacked_ref[...], preferred_element_type=F32)


def term_kernel(me_ref, slot_ref, mpo_ref, left_hbm, site_ref, *rest, groups):
    added = sum(offset is not None for _, _, offset in groups)
    others, outs = list(rest[:added]), rest[added : added + len(groups)]
    left_ref, mix_ref, stacked_ref, inverse_ref, left_sem = rest[added + len(groups) :]
    wslices = left_ref.shape[1]
    columns = site_ref.shape[2]
    chip, core = lax.div(me_ref[0], 2), lax.rem(me_ref[0], 2)
    for k in range(slot_ref.shape[0]):
        inverse_ref[slot_ref[k]] = k
    work = []
    for g, (targets, _, offset) in enumerate(groups):
        other = None if offset is None else others.pop(0)
        for j, (step, flip) in enumerate(targets):
            member = 2 * lax.rem(chip + step, CHIPS) + (1 - core if flip else core)
            parts = []
            for b in range(2):
                n = 2 * len(work) + b
                sector = inverse_ref[2 * member + b]
                copy = pltpu.make_async_copy(left_hbm.at[sector], left_ref.at[n], left_sem.at[n])
                copy.start()
                parts.append((copy, sector))
            work.append((parts, outs[g], other, offset, 2 * j))
    mixing_matrix(mpo_ref, mix_ref, wslices, PHYS, columns // PHYS)
    for i, (parts, out_ref, other_ref, offset, start) in enumerate(work):
        for copy, _ in parts:
            copy.wait()
        for b, (_, sector) in enumerate(parts):
            mix(site_ref[sector], mix_ref, stacked_ref.at[b])
        for b in range(2):
            term = contract(left_ref.at[2 * i + b], stacked_ref.at[b])
            if other_ref is not None:
                term = term + other_ref[offset + start + b].astype(F32)
            out_ref[start + b] = term.astype(out_ref.dtype)


def terms(me, slots, mpo_flat, left_env, site, *groups):
    sectors, wslices, rows, _ = left_env.shape
    columns = site.shape[2]
    count = 2 * sum(len(targets) for targets, _, _ in groups)
    vmem = pl.BlockSpec(memory_space=pltpu.VMEM)
    smem = pl.BlockSpec(memory_space=pltpu.SMEM)
    hbm = pl.BlockSpec(memory_space=pltpu.HBM)
    others = [other[0] for _, _, other in groups if other is not None]
    flops = 2 * count * rows * columns * wslices * (rows + columns)
    moved = count * (wslices * rows * rows * 2 + rows * columns * 2)
    return pl.pallas_call(
        functools.partial(
            term_kernel,
            groups=[(targets, dtype, other and other[1]) for targets, dtype, other in groups],
        ),
        out_shape=[
            jax.ShapeDtypeStruct((2 * len(targets), rows, columns), dtype)
            for targets, dtype, _ in groups
        ],
        in_specs=[smem, smem, smem, hbm, vmem] + [vmem] * len(others),
        out_specs=[vmem] * len(groups),
        scratch_shapes=[
            pltpu.VMEM((count, wslices, rows, rows), BF16),
            pltpu.VMEM((columns, wslices * columns), BF16),
            pltpu.VMEM((2, wslices * rows, columns), BF16),
            pltpu.SMEM((sectors,), jnp.int32),
            pltpu.SemaphoreType.DMA((count,)),
        ],
        compiler_params=pltpu.CompilerParams(vmem_limit_bytes=TERM_MIB * 2**20),
        cost_estimate=pl.CostEstimate(flops=flops, bytes_accessed=moved, transcendentals=0),
    )(me, slots, mpo_flat, left_env, site, *others)


def split(a):
    high = a.astype(BF16)
    return high, (a - high.astype(F32)).astype(BF16)


def product(a, b):
    return jnp.dot(
        jnp.concatenate([a[0], a[0], a[1]], axis=1),
        jnp.concatenate([b[0], b[1], b[0]], axis=0),
        preferred_element_type=F32,
    )


def root_kernel(own_ref, other_ref, far_ref, up_ref, down_ref, out_ref):
    count, rows, columns = far_ref.shape
    parts, _, part_rows, _ = out_ref.shape
    eye = lax.broadcasted_iota(jnp.int32, (columns, columns), 0) == lax.broadcasted_iota(
        jnp.int32, (columns, columns), 1
    )
    identity = eye.astype(F32)
    sectors = range(count)
    term, current, scale = [], [], []
    for b in sectors:
        total = (
            own_ref[b]
            + other_ref[b].astype(F32)
            + far_ref[b].astype(F32)
            + up_ref[b].astype(F32)
            + down_ref[b].astype(F32)
        )
        high, low = split(total)
        gram = lax.dot_general(
            jnp.concatenate([high, high, low], axis=0),
            jnp.concatenate([high, low, high], axis=0),
            (((0,), (0,)), ((), ())),
            preferred_element_type=F32,
        )
        norm = jnp.sqrt(jnp.sum(gram * gram, keepdims=True))
        term.append((high, low))
        current.append(gram / norm)
        scale.append(1.0 / jnp.sqrt(norm))
    partner = [None] * count
    for repeat in range(ITERS):
        if repeat < EARLY:
            rounded = [current[b].astype(BF16) for b in sectors]
            if repeat == 0:
                step = current
            else:
                others = [partner[b].astype(BF16) for b in sectors]
                step = [
                    jnp.dot(others[b], rounded[b], preferred_element_type=F32) for b in sectors
                ]
            small = [step[b].astype(BF16) for b in sectors]
            current = [
                1.5 * current[b]
                - 0.5 * jnp.dot(rounded[b], small[b], preferred_element_type=F32)
                for b in sectors
            ]
            if repeat == 0:
                partner = [1.5 * identity - 0.5 * step[b] for b in sectors]
            else:
                partner = [
                    1.5 * partner[b]
                    - 0.5 * jnp.dot(small[b], others[b], preferred_element_type=F32)
                    for b in sectors
                ]
        else:
            rounded = [current[b].astype(BF16) for b in sectors]
            others = [partner[b].astype(BF16) for b in sectors]
            away = [
                (
                    0.5 * identity
                    - 0.5 * jnp.dot(others[b], rounded[b], preferred_element_type=F32)
                ).astype(BF16)
                for b in sectors
            ]
            if repeat < ITERS - 1:
                current = [
                    current[b] + jnp.dot(rounded[b], away[b], preferred_element_type=F32)
                    for b in sectors
                ]
            partner = [
                partner[b] + jnp.dot(away[b], others[b], preferred_element_type=F32)
                for b in sectors
            ]
    for b in sectors:
        result = (product(term[b], split(partner[b] * scale[b]))).astype(BF16)
        for m in range(parts):
            out_ref[m, b] = result[m * part_rows : (m + 1) * part_rows]


def expansions(own, other, far, up, down, parts):
    count, rows, columns = far.shape
    flops = 2 * 3 * count * columns * columns * (15 * columns + 2 * rows)
    return pl.pallas_call(
        root_kernel,
        out_shape=jax.ShapeDtypeStruct((parts, count, rows // parts, columns), BF16),
        in_specs=[pl.BlockSpec(memory_space=pltpu.VMEM)] * 5,
        out_specs=pl.BlockSpec(memory_space=pltpu.VMEM),
        compiler_params=pltpu.CompilerParams(vmem_limit_bytes=40 * 2**20),
        cost_estimate=pl.CostEstimate(
            flops=flops, bytes_accessed=count * rows * columns * 12, transcendentals=0
        ),
    )(own, other, far, up, down)


def shards(left_env, site_tensor, mpo_column, sector_slot, kept):
    columns = site_tensor.shape[2]
    members = lax.axis_size("mpo")
    me = lax.axis_index("mpo").reshape(1)
    swap = [(2 * c + q, 2 * c + 1 - q) for c in range(CHIPS) for q in range(2)]

    def shift(step):
        return [
            (2 * c + q, 2 * ((c + step) % CHIPS) + q) for c in range(CHIPS) for q in range(2)
        ]

    flat = mpo_column.astype(F32).reshape(-1)
    after = lax.optimization_barrier

    def run(slots, *groups):
        return terms(me, slots, flat, left_env, site_tensor, *groups)

    far_other, near_other, far_own = run(
        sector_slot,
        ([(2, 1)], BF16, None),
        ([(1, 1), (3, 1)], BF16, None),
        ([(2, 0)], F32, None),
    )
    far_other = lax.ppermute(far_other, "mpo", swap)
    near_other, far_other = after((near_other, far_other))
    near_other = lax.ppermute(near_other, "mpo", swap)
    far = (far_own + far_other.astype(F32)).astype(BF16)
    far = lax.ppermute(far, "mpo", shift(2))
    up, down, own_other = run(
        sector_slot,
        ([(1, 0)], BF16, (near_other, 0)),
        ([(3, 0)], BF16, (near_other, 2)),
        ([(0, 1)], BF16, None),
    )
    up, slots = after((up, sector_slot))
    up = lax.ppermute(up, "mpo", shift(1))
    down = lax.ppermute(down, "mpo", shift(3))
    own_other = lax.ppermute(own_other, "mpo", swap)
    (own,) = run(slots, ([(0, 0)], F32, None))
    result = expansions(own, own_other, far, up, down, members)
    rows = lax.all_to_all(result, "mpo", split_axis=0, concat_axis=0, tiled=True)
    rows = rows.reshape(-1, rows.shape[2], columns)
    routed = lax.all_to_all(rows, "sec", split_axis=0, concat_axis=0, tiled=True)
    keep = jnp.arange(columns, dtype=jnp.int32)[None, None, :] < kept[:, None, None]
    return jnp.where(keep, routed, jnp.zeros((), BF16))


def solution(mesh):
    return jax.shard_map(
        shards,
        mesh=mesh,
        in_specs=(
            P("sec", "mpo", None, None),
            P("sec", None, None),
            P("mpo", None, None),
            P("sec"),
            P("sec"),
        ),
        out_specs=P("sec", "mpo", None),
        check_vma=False,
    )
```

```python
import functools

import jax
import jax.numpy as jnp
from jax import lax
from jax.experimental import pallas as pl
from jax.experimental.pallas import tpu as pltpu
from jax.sharding import PartitionSpec as P

ITERS = 6
EARLY = 4
PHYS = 4
CHIPS = 4
TERM_MIB = 48
F32, BF16 = jnp.float32, jnp.bfloat16


def mixing_matrix(mpo_ref, out_ref, wslices, phys, right):
    per = 128 // right
    row = lax.broadcasted_iota(jnp.int32, (right, 128), 0)
    lane = lax.broadcasted_iota(jnp.int32, (right, 128), 1)
    for s in range(phys):
        for w in range(wslices):
            for t in range(0, phys, per):
                block = jnp.zeros((right, 128), F32)
                for p in range(per):
                    value = mpo_ref[(w * phys + s) * phys + t + p]
                    block = jnp.where(lane == row + p * right, value, block)
                column = (w * phys + t) * right
                out_ref[s * right : (s + 1) * right, column : column + 128] = block.astype(BF16)


def mix(site, mix_ref, stacked_ref):
    rows, columns = site.shape
    for w in range(stacked_ref.shape[0] // rows):
        stacked_ref[w * rows : (w + 1) * rows] = jnp.dot(
            site, mix_ref[:, w * columns : (w + 1) * columns], preferred_element_type=F32
        ).astype(BF16)


def contract(left_ref, stacked_ref):
    left = jnp.concatenate([left_ref[w] for w in range(left_ref.shape[0])], axis=1)
    return jnp.dot(left, stacked_ref[...], preferred_element_type=F32)


def term_kernel(me_ref, slot_ref, mpo_ref, left_hbm, site_ref, *rest, groups):
    added = sum(offset is not None for _, _, offset in groups)
    others, outs = list(rest[:added]), rest[added : added + len(groups)]
    left_ref, mix_ref, stacked_ref, inverse_ref, left_sem = rest[added + len(groups) :]
    wslices = left_ref.shape[1]
    columns = site_ref.shape[2]
    chip, core = lax.div(me_ref[0], 2), lax.rem(me_ref[0], 2)
    for k in range(slot_ref.shape[0]):
        inverse_ref[slot_ref[k]] = k
    work = []
    for g, (targets, _, offset) in enumerate(groups):
        other = None if offset is None else others.pop(0)
        for j, (step, flip) in enumerate(targets):
            member = 2 * lax.rem(chip + step, CHIPS) + (1 - core if flip else core)
            parts = []
            for b in range(2):
                n = 2 * len(work) + b
                sector = inverse_ref[2 * member + b]
                copy = pltpu.make_async_copy(left_hbm.at[sector], left_ref.at[n], left_sem.at[n])
                copy.start()
                parts.append((copy, sector))
            work.append((parts, outs[g], other, offset, 2 * j))
    mixing_matrix(mpo_ref, mix_ref, wslices, PHYS, columns // PHYS)
    for i, (parts, out_ref, other_ref, offset, start) in enumerate(work):
        for copy, _ in parts:
            copy.wait()
        for b, (_, sector) in enumerate(parts):
            mix(site_ref[sector], mix_ref, stacked_ref.at[b])
        for b in range(2):
            term = contract(left_ref.at[2 * i + b], stacked_ref.at[b])
            if other_ref is not None:
                term = term + other_ref[offset + start + b].astype(F32)
            out_ref[start + b] = term.astype(out_ref.dtype)


def terms(me, slots, mpo_flat, left_env, site, *groups):
    sectors, wslices, rows, _ = left_env.shape
    columns = site.shape[2]
    count = 2 * sum(len(targets) for targets, _, _ in groups)
    vmem = pl.BlockSpec(memory_space=pltpu.VMEM)
    smem = pl.BlockSpec(memory_space=pltpu.SMEM)
    hbm = pl.BlockSpec(memory_space=pltpu.HBM)
    others = [other[0] for _, _, other in groups if other is not None]
    flops = 2 * count * rows * columns * wslices * (rows + columns)
    moved = count * (wslices * rows * rows * 2 + rows * columns * 2)
    return pl.pallas_call(
        functools.partial(
            term_kernel,
            groups=[(targets, dtype, other and other[1]) for targets, dtype, other in groups],
        ),
        out_shape=[
            jax.ShapeDtypeStruct((2 * len(targets), rows, columns), dtype)
            for targets, dtype, _ in groups
        ],
        in_specs=[smem, smem, smem, hbm, vmem] + [vmem] * len(others),
        out_specs=[vmem] * len(groups),
        scratch_shapes=[
            pltpu.VMEM((count, wslices, rows, rows), BF16),
            pltpu.VMEM((columns, wslices * columns), BF16),
            pltpu.VMEM((2, wslices * rows, columns), BF16),
            pltpu.SMEM((sectors,), jnp.int32),
            pltpu.SemaphoreType.DMA((count,)),
        ],
        compiler_params=pltpu.CompilerParams(vmem_limit_bytes=TERM_MIB * 2**20),
        cost_estimate=pl.CostEstimate(flops=flops, bytes_accessed=moved, transcendentals=0),
    )(me, slots, mpo_flat, left_env, site, *others)


def split(a):
    high = a.astype(BF16)
    return high, (a - high.astype(F32)).astype(BF16)


def product(a, b):
    return jnp.dot(
        jnp.concatenate([a[0], a[0], a[1]], axis=1),
        jnp.concatenate([b[0], b[1], b[0]], axis=0),
        preferred_element_type=F32,
    )


def root_kernel(own_ref, other_ref, far_ref, up_ref, down_ref, out_ref):
    count, rows, columns = far_ref.shape
    parts, _, part_rows, _ = out_ref.shape
    eye = lax.broadcasted_iota(jnp.int32, (columns, columns), 0) == lax.broadcasted_iota(
        jnp.int32, (columns, columns), 1
    )
    identity = eye.astype(F32)
    sectors = range(count)
    term, current, scale = [], [], []
    for b in sectors:
        total = (
            own_ref[b]
            + other_ref[b].astype(F32)
            + far_ref[b].astype(F32)
            + up_ref[b].astype(F32)
            + down_ref[b].astype(F32)
        )
        high, low = split(total)
        both = lax.dot_general(
            high,
            jnp.concatenate([high, low], axis=1),
            (((0,), (0,)), ((), ())),
            preferred_element_type=F32,
        )
        cross = both[:, columns:]
        gram = both[:, :columns] + (cross + cross.T)
        norm = jnp.sqrt(jnp.sum(gram * gram, keepdims=True))
        term.append((high, low))
        current.append(gram / norm)
        scale.append(1.0 / jnp.sqrt(norm))
    partner = [None] * count
    for repeat in range(ITERS):
        if repeat < EARLY:
            rounded = [current[b].astype(BF16) for b in sectors]
            if repeat == 0:
                step = current
            else:
                others = [partner[b].astype(BF16) for b in sectors]
                step = [
                    jnp.dot(others[b], rounded[b], preferred_element_type=F32) for b in sectors
                ]
            small = [step[b].astype(BF16) for b in sectors]
            current = [
                1.5 * current[b]
                - 0.5 * jnp.dot(rounded[b], small[b], preferred_element_type=F32)
                for b in sectors
            ]
            if repeat == 0:
                partner = [1.5 * identity - 0.5 * step[b] for b in sectors]
            else:
                partner = [
                    1.5 * partner[b]
                    - 0.5 * jnp.dot(small[b], others[b], preferred_element_type=F32)
                    for b in sectors
                ]
        else:
            rounded = [current[b].astype(BF16) for b in sectors]
            others = [partner[b].astype(BF16) for b in sectors]
            away = [
                (
                    0.5 * identity
                    - 0.5 * jnp.dot(others[b], rounded[b], preferred_element_type=F32)
                ).astype(BF16)
                for b in sectors
            ]
            if repeat < ITERS - 1:
                current = [
                    current[b] + jnp.dot(rounded[b], away[b], preferred_element_type=F32)
                    for b in sectors
                ]
            partner = [
                partner[b] + jnp.dot(away[b], others[b], preferred_element_type=F32)
                for b in sectors
            ]
    for b in sectors:
        result = (product(term[b], split(partner[b] * scale[b]))).astype(BF16)
        for m in range(parts):
            out_ref[m, b] = result[m * part_rows : (m + 1) * part_rows]


def expansions(own, other, far, up, down, parts):
    count, rows, columns = far.shape
    flops = 2 * 3 * count * columns * columns * (15 * columns + 2 * rows)
    return pl.pallas_call(
        root_kernel,
        out_shape=jax.ShapeDtypeStruct((parts, count, rows // parts, columns), BF16),
        in_specs=[pl.BlockSpec(memory_space=pltpu.VMEM)] * 5,
        out_specs=pl.BlockSpec(memory_space=pltpu.VMEM),
        compiler_params=pltpu.CompilerParams(vmem_limit_bytes=40 * 2**20),
        cost_estimate=pl.CostEstimate(
            flops=flops, bytes_accessed=count * rows * columns * 12, transcendentals=0
        ),
    )(own, other, far, up, down)


def shards(left_env, site_tensor, mpo_column, sector_slot, kept):
    columns = site_tensor.shape[2]
    members = lax.axis_size("mpo")
    me = lax.axis_index("mpo").reshape(1)
    swap = [(2 * c + q, 2 * c + 1 - q) for c in range(CHIPS) for q in range(2)]

    def shift(step):
        return [
            (2 * c + q, 2 * ((c + step) % CHIPS) + q) for c in range(CHIPS) for q in range(2)
        ]

    flat = mpo_column.astype(F32).reshape(-1)
    after = lax.optimization_barrier

    def run(slots, *groups):
        return terms(me, slots, flat, left_env, site_tensor, *groups)

    far_other, near_other, far_own = run(
        sector_slot,
        ([(2, 1)], BF16, None),
        ([(1, 1), (3, 1)], BF16, None),
        ([(2, 0)], F32, None),
    )
    far_other = lax.ppermute(far_other, "mpo", swap)
    near_other, far_other = after((near_other, far_other))
    near_other = lax.ppermute(near_other, "mpo", swap)
    far = (far_own + far_other.astype(F32)).astype(BF16)
    far = lax.ppermute(far, "mpo", shift(2))
    up, down, own_other = run(
        sector_slot,
        ([(1, 0)], BF16, (near_other, 0)),
        ([(3, 0)], BF16, (near_other, 2)),
        ([(0, 1)], BF16, None),
    )
    up, slots = after((up, sector_slot))
    up = lax.ppermute(up, "mpo", shift(1))
    down = lax.ppermute(down, "mpo", shift(3))
    own_other = lax.ppermute(own_other, "mpo", swap)
    (own,) = run(slots, ([(0, 0)], F32, None))
    result = expansions(own, own_other, far, up, down, members)
    rows = lax.all_to_all(result, "mpo", split_axis=0, concat_axis=0, tiled=True)
    rows = rows.reshape(-1, rows.shape[2], columns)
    routed = lax.all_to_all(rows, "sec", split_axis=0, concat_axis=0, tiled=True)
    keep = jnp.arange(columns, dtype=jnp.int32)[None, None, :] < kept[:, None, None]
    return jnp.where(keep, routed, jnp.zeros((), BF16))


def solution(mesh):
    return jax.shard_map(
        shards,
        mesh=mesh,
        in_specs=(
            P("sec", "mpo", None, None),
            P("sec", None, None),
            P("mpo", None, None),
            P("sec"),
            P("sec"),
        ),
        out_specs=P("sec", "mpo", None),
        check_vma=False,
    )
```

```python
import functools

import jax
import jax.numpy as jnp
from jax import lax
from jax.experimental import pallas as pl
from jax.experimental.pallas import tpu as pltpu
from jax.sharding import PartitionSpec as P

ITERS = 6
EARLY = 4
PHYS = 4
CHIPS = 4
TERM_MIB = 48
F32, BF16 = jnp.float32, jnp.bfloat16


def mixing_matrix(mpo_ref, out_ref, wslices, phys, right):
    per = 128 // right
    row = lax.broadcasted_iota(jnp.int32, (right, 128), 0)
    lane = lax.broadcasted_iota(jnp.int32, (right, 128), 1)
    for s in range(phys):
        for w in range(wslices):
            for t in range(0, phys, per):
                block = jnp.zeros((right, 128), F32)
                for p in range(per):
                    value = mpo_ref[(w * phys + s) * phys + t + p]
                    block = jnp.where(lane == row + p * right, value, block)
                column = (w * phys + t) * right
                out_ref[s * right : (s + 1) * right, column : column + 128] = block.astype(BF16)


def mix(site, mix_ref, stacked_ref):
    rows, columns = site.shape
    for w in range(stacked_ref.shape[0] // rows):
        stacked_ref[w * rows : (w + 1) * rows] = jnp.dot(
            site, mix_ref[:, w * columns : (w + 1) * columns], preferred_element_type=F32
        ).astype(BF16)


def contract(left_ref, stacked_ref):
    left = jnp.concatenate([left_ref[w] for w in range(left_ref.shape[0])], axis=1)
    return jnp.dot(left, stacked_ref[...], preferred_element_type=F32)


def term_kernel(me_ref, slot_ref, mpo_ref, left_hbm, site_ref, *rest, groups):
    added = sum(offset is not None for _, _, offset in groups)
    others, outs = list(rest[:added]), rest[added : added + len(groups)]
    left_ref, mix_ref, stacked_ref, inverse_ref, left_sem = rest[added + len(groups) :]
    wslices = left_ref.shape[1]
    columns = site_ref.shape[2]
    chip, core = lax.div(me_ref[0], 2), lax.rem(me_ref[0], 2)
    for k in range(slot_ref.shape[0]):
        inverse_ref[slot_ref[k]] = k
    work = []
    for g, (targets, _, offset) in enumerate(groups):
        other = None if offset is None else others.pop(0)
        for j, (step, flip) in enumerate(targets):
            member = 2 * lax.rem(chip + step, CHIPS) + (1 - core if flip else core)
            parts = []
            for b in range(2):
                n = 2 * len(work) + b
                sector = inverse_ref[2 * member + b]
                copy = pltpu.make_async_copy(left_hbm.at[sector], left_ref.at[n], left_sem.at[n])
                copy.start()
                parts.append((copy, sector))
            work.append((parts, outs[g], other, offset, 2 * j))
    mixing_matrix(mpo_ref, mix_ref, wslices, PHYS, columns // PHYS)
    for i, (parts, out_ref, other_ref, offset, start) in enumerate(work):
        for copy, _ in parts:
            copy.wait()
        for b, (_, sector) in enumerate(parts):
            mix(site_ref[sector], mix_ref, stacked_ref.at[b])
        for b in range(2):
            term = contract(left_ref.at[2 * i + b], stacked_ref.at[b])
            if other_ref is not None:
                term = term + other_ref[offset + start + b].astype(F32)
            out_ref[start + b] = term.astype(out_ref.dtype)


def terms(me, slots, mpo_flat, left_env, site, *groups):
    sectors, wslices, rows, _ = left_env.shape
    columns = site.shape[2]
    count = 2 * sum(len(targets) for targets, _, _ in groups)
    vmem = pl.BlockSpec(memory_space=pltpu.VMEM)
    smem = pl.BlockSpec(memory_space=pltpu.SMEM)
    hbm = pl.BlockSpec(memory_space=pltpu.HBM)
    others = [other[0] for _, _, other in groups if other is not None]
    flops = 2 * count * rows * columns * wslices * (rows + columns)
    moved = count * (wslices * rows * rows * 2 + rows * columns * 2)
    return pl.pallas_call(
        functools.partial(
            term_kernel,
            groups=[(targets, dtype, other and other[1]) for targets, dtype, other in groups],
        ),
        out_shape=[
            jax.ShapeDtypeStruct((2 * len(targets), rows, columns), dtype)
            for targets, dtype, _ in groups
        ],
        in_specs=[smem, smem, smem, hbm, vmem] + [vmem] * len(others),
        out_specs=[vmem] * len(groups),
        scratch_shapes=[
            pltpu.VMEM((count, wslices, rows, rows), BF16),
            pltpu.VMEM((columns, wslices * columns), BF16),
            pltpu.VMEM((2, wslices * rows, columns), BF16),
            pltpu.SMEM((sectors,), jnp.int32),
            pltpu.SemaphoreType.DMA((count,)),
        ],
        compiler_params=pltpu.CompilerParams(vmem_limit_bytes=TERM_MIB * 2**20),
        cost_estimate=pl.CostEstimate(flops=flops, bytes_accessed=moved, transcendentals=0),
    )(me, slots, mpo_flat, left_env, site, *others)


def split(a):
    high = a.astype(BF16)
    return high, (a - high.astype(F32)).astype(BF16)


def product(a, b):
    return jnp.dot(
        jnp.concatenate([a[0], a[0], a[1]], axis=1),
        jnp.concatenate([b[0], b[1], b[0]], axis=0),
        preferred_element_type=F32,
    )


def root_kernel(own_ref, other_ref, far_ref, up_ref, down_ref, out_ref):
    count, rows, columns = far_ref.shape
    parts, _, part_rows, _ = out_ref.shape
    eye = lax.broadcasted_iota(jnp.int32, (columns, columns), 0) == lax.broadcasted_iota(
        jnp.int32, (columns, columns), 1
    )
    identity = eye.astype(F32)
    sectors = range(count)
    term, current, scale = [], [], []
    for b in sectors:
        total = (
            own_ref[b]
            + other_ref[b].astype(F32)
            + far_ref[b].astype(F32)
            + up_ref[b].astype(F32)
            + down_ref[b].astype(F32)
        )
        high, low = split(total)
        both = lax.dot_general(
            high,
            jnp.concatenate([high, low], axis=1),
            (((0,), (0,)), ((), ())),
            preferred_element_type=F32,
        )
        cross = both[:, columns:]
        gram = both[:, :columns] + (cross + cross.T)
        norm = jnp.sqrt(jnp.sum(gram * gram, keepdims=True))
        term.append((high, low))
        current.append(gram / norm)
        scale.append(1.0 / jnp.sqrt(norm))
    partner = [None] * count
    for repeat in range(ITERS):
        if repeat < EARLY:
            rounded = [current[b].astype(BF16) for b in sectors]
            if repeat == 0:
                step = current
            else:
                others = [partner[b].astype(BF16) for b in sectors]
                step = [
                    jnp.dot(others[b], rounded[b], preferred_element_type=F32) for b in sectors
                ]
            small = [step[b].astype(BF16) for b in sectors]
            current = [
                1.5 * current[b]
                - 0.5 * jnp.dot(rounded[b], small[b], preferred_element_type=F32)
                for b in sectors
            ]
            if repeat == 0:
                partner = [1.5 * identity - 0.5 * step[b] for b in sectors]
            else:
                partner = [
                    1.5 * partner[b]
                    - 0.5 * jnp.dot(small[b], others[b], preferred_element_type=F32)
                    for b in sectors
                ]
        else:
            rounded = [current[b].astype(BF16) for b in sectors]
            others = [partner[b].astype(BF16) for b in sectors]
            away = [
                (
                    0.5 * identity
                    - 0.5 * jnp.dot(others[b], rounded[b], preferred_element_type=F32)
                ).astype(BF16)
                for b in sectors
            ]
            if repeat < ITERS - 1:
                current = [
                    current[b] + jnp.dot(rounded[b], away[b], preferred_element_type=F32)
                    for b in sectors
                ]
            partner = [
                partner[b] + jnp.dot(away[b], others[b], preferred_element_type=F32)
                for b in sectors
            ]
    for b in sectors:
        result = (product(term[b], split(partner[b] * scale[b]))).astype(BF16)
        for m in range(parts):
            out_ref[m, b] = result[m * part_rows : (m + 1) * part_rows]


def expansions(own, other, far, up, down, parts):
    count, rows, columns = far.shape
    flops = 2 * 3 * count * columns * columns * (15 * columns + 2 * rows)
    return pl.pallas_call(
        root_kernel,
        out_shape=jax.ShapeDtypeStruct((parts, count, rows // parts, columns), BF16),
        in_specs=[pl.BlockSpec(memory_space=pltpu.VMEM)] * 5,
        out_specs=pl.BlockSpec(memory_space=pltpu.VMEM),
        compiler_params=pltpu.CompilerParams(vmem_limit_bytes=40 * 2**20),
        cost_estimate=pl.CostEstimate(
            flops=flops, bytes_accessed=count * rows * columns * 12, transcendentals=0
        ),
    )(own, other, far, up, down)


def shards(left_env, site_tensor, mpo_column, sector_slot, kept):
    columns = site_tensor.shape[2]
    members = lax.axis_size("mpo")
    me = lax.axis_index("mpo").reshape(1)
    swap = [(2 * c + q, 2 * c + 1 - q) for c in range(CHIPS) for q in range(2)]

    def shift(step):
        return [
            (2 * c + q, 2 * ((c + step) % CHIPS) + q) for c in range(CHIPS) for q in range(2)
        ]

    flat = mpo_column.astype(F32).reshape(-1)
    after = lax.optimization_barrier

    def run(slots, *groups):
        return terms(me, slots, flat, left_env, site_tensor, *groups)

    far_other, near_other, far_own = run(
        sector_slot,
        ([(2, 1)], BF16, None),
        ([(1, 1), (3, 1)], BF16, None),
        ([(2, 0)], F32, None),
    )
    far_other = lax.ppermute(far_other, "mpo", swap)
    near_other, far_other = after((near_other, far_other))
    near_other = lax.ppermute(near_other, "mpo", swap)
    far = (far_own + far_other.astype(F32)).astype(BF16)
    far = lax.ppermute(far, "mpo", shift(2))
    up, down, own_other = run(
        sector_slot,
        ([(1, 0)], BF16, (near_other, 0)),
        ([(3, 0)], BF16, (near_other, 2)),
        ([(0, 1)], BF16, None),
    )
    up, slots = after((up, sector_slot))
    up = lax.ppermute(up, "mpo", shift(1))
    down = lax.ppermute(down, "mpo", shift(3))
    own_other = lax.ppermute(own_other, "mpo", swap)
    (own,) = run(slots, ([(0, 0)], F32, None))
    result = expansions(own, own_other, far, up, down, members)
    rows = lax.all_to_all(result, "mpo", split_axis=0, concat_axis=0, tiled=True)
    rows = rows.reshape(-1, rows.shape[2], columns)
    routed = lax.all_to_all(rows, "sec", split_axis=0, concat_axis=0, tiled=True)
    routed, kept = lax.optimization_barrier((routed, kept))
    keep = jnp.arange(columns, dtype=jnp.int32)[None, None, :] < kept[:, None, None]
    return jnp.where(keep, routed, jnp.zeros((), BF16))


def solution(mesh):
    return jax.shard_map(
        shards,
        mesh=mesh,
        in_specs=(
            P("sec", "mpo", None, None),
            P("sec", None, None),
            P("mpo", None, None),
            P("sec"),
            P("sec"),
        ),
        out_specs=P("sec", "mpo", None),
        check_vma=False,
    )
```
